128 devices in a mesh: dp: 64 (over z_hi, x, y, core), tensor: 2 (over z_lo).
Axes of the slice: x: 4, y: 4, z: 4 (z_hi: 2, z_lo: 2; z = z_hi * 2 + z_lo), core: 2. Of those that a mesh axis runs over, the one named last changes fastest.
Arguments:
- layer_input: bfloat16 [32768, 768], P('dp'), may hold values from -6 to 6
- seg_ids: int32 [32768], P('dp'), may hold values from 0 to 127, never falling along the last dimension, each value on 1 to 2048 neighbouring positions
- ln1_gain: float32 [768], replicated, may hold values from 0.5 to 1.5
- ln1_bias: float32 [768], replicated, may hold values from -2.5 to 2.5
- ln2_gain: float32 [768], replicated, may hold values from 0.5 to 1.5
- ln2_bias: float32 [768], replicated, may hold values from -2.5 to 2.5
- w_qkv: bfloat16 [768, 12, 192], P(None, 'tensor'), may hold values from -0.21875 to 0.21875
- b_qkv: float32 [12, 192], P('tensor'), may hold values from -2.5 to 2.5
- w_out: bfloat16 [12, 64, 768], P('tensor'), may hold values from -0.625 to 0.625
- b_out: float32 [768], replicated, may hold values from -2.5 to 2.5
- w_fc: bfloat16 [768, 3072], P(None, 'tensor'), may hold values from -0.21875 to 0.21875
- b_fc: float32 [3072], P('tensor'), may hold values from -2.5 to 2.5
- w_proj: bfloat16 [3072, 768], P('tensor'), may hold values from -0.109375 to 0.109375
- b_proj: float32 [768], replicated, may hold values from -2.5 to 2.5
- cotangent: float32 [32768, 768], P('dp'), may hold values from -6 to 6
Outputs:
- layer_output: bfloat16 [32768, 768], P('dp')
- grad_input: float32 [32768, 768], P('dp')
- grad_ln1_gain: float32 [768], replicated
- grad_ln1_bias: float32 [768], replicated
- grad_ln2_gain: float32 [768], replicated
- grad_ln2_bias: float32 [768], replicated
- grad_w_qkv: float32 [768, 12, 192], P(None, 'tensor')
- grad_b_qkv: float32 [12, 192], P('tensor')
- grad_w_out: float32 [12, 64, 768], P('tensor')
- grad_b_out: float32 [768], replicated
- grad_w_fc: float32 [768, 3072], P(None, 'tensor')
- grad_b_fc: float32 [3072], P('tensor')
- grad_w_proj: float32 [3072, 768], P('tensor')
- grad_b_proj: float32 [768], replicated
The draws below stay inside these ranges and needn't reach their ends.
Inputs may be any that keep to these rules, and one draw needn't show every extreme that they name: `seg_ids`: document numbers never fall from one token to the next.
All inputs are finite; a program needn't handle non-finite values.
Results may differ from the reference program's by a relative error of at most 0.0098.
Values may be sent and summed in bfloat16 or wider, within the bound.
No kernel may reach another device: no remote copies, remote signals or barrier semaphores. Data moves between devices by JAX's collectives and lax.ppermute only.
A program may use at most 128 MiB of HBM per device.

```python
import math
import jax
import jax.numpy as jnp
import numpy as np
from jax import lax

D = 768
H = 12
HD = 64
ROT = 16
FF = 3072
SEQ = 512
TOKENS = 32768


def steps_of(own_key, dims, split, smallest, high):
    loudness, own = 1.0, jax.random.fold_in(own_key, 6)
    for axis_at, blocks in split:
        steps = jnp.exp(jax.random.uniform(jax.random.fold_in(own, axis_at), (blocks,), jnp.float32, smallest / len(split), high / len(split)))
        loudness = loudness * jnp.repeat(steps, dims[axis_at] // blocks).reshape([-1 if axis == axis_at else 1 for axis in range(len(dims))])
    return loudness


def split_up(amount, total, most, skew):
    portions = [(1 << 20) // math.isqrt(grade ** skew) + 1 for grade in range(2, amount + 1)]
    surplus, given = total - most - (amount - 1), [1] * (amount - 1)
    while surplus > 0:
        candidates = [i for i in range(amount - 1) if given[i] < most]
        mass, left = sum([portions[i] for i in candidates]), surplus
        for i in candidates:
            extra = min(most - given[i], max(1, left * portions[i] // mass), surplus)
            given[i] = given[i] + extra
            surplus = surplus - extra
    return np.array([most] + given)


def ragged_sizes(key, count, total, reach, lean):
    if count == 2:
        one = jax.random.randint(key, (), max(1, total - reach), min(reach, total - 1) + 1)
        return jnp.stack([one, total - one])
    tallies = jnp.asarray(split_up(count, total, reach, lean), jnp.int32)
    couples = (count - 1) // 2
    giver, sink = tallies[1:1 + 2 * couples:2], tallies[2:2 + 2 * couples:2]
    margin = jnp.minimum(giver - 1, reach - sink)
    passed = jax.random.randint(jax.random.fold_in(key, 1), (couples,), 0, 1 << 20) % (margin + 1)
    tallies = tallies.at[1:1 + 2 * couples:2].set(giver - passed).at[2:2 + 2 * couples:2].set(sink + passed)
    return tallies[jax.random.permutation(jax.random.fold_in(key, 2), count)]


def noise(own_key, shape, width, bound, split=(), kind=jnp.bfloat16):
    entries = width * jax.random.normal(own_key, shape, jnp.float32)
    if split:
        entries = entries * steps_of(own_key, shape, split, -0.22, 0.18)
    return jnp.clip(entries, -bound, bound).astype(kind)


def setup_inputs(seed: int = 0) -> dict:
    key_of = jax.random.split(jax.random.key(seed), 16)
    layer_input = noise(key_of[0], (TOKENS, D), 1.0, 6.0, ((0, 64),))
    seg_ids = jnp.searchsorted(jnp.cumsum(ragged_sizes(key_of[1], 2 * TOKENS // SEQ, TOKENS, 4 * SEQ, 0)), jnp.arange(TOKENS), side="right").astype(jnp.int32)
    ln1_gain = jnp.clip(1.0 + 0.1 * jax.random.normal(key_of[2], (D,), jnp.float32), 0.5, 1.5)
    ln1_bias = noise(key_of[3], (D,), 0.3, 2.5, (), jnp.float32)
    ln2_gain = jnp.clip(1.0 + 0.1 * jax.random.normal(key_of[4], (D,), jnp.float32), 0.5, 1.5)
    ln2_bias = noise(key_of[5], (D,), 0.3, 2.5, (), jnp.float32)
    w_qkv = noise(key_of[6], (D, H, 3 * HD), D ** -0.5, 0.21875, ((1, 2),))
    b_qkv = noise(key_of[7], (H, 3 * HD), 0.3, 2.5, ((0, 2),), jnp.float32)
    w_out = noise(key_of[8], (H, HD, D), (D // 8) ** -0.5, 0.625, ((0, 2),))
    b_out = noise(key_of[9], (D,), 0.3, 2.5, (), jnp.float32)
    w_fc = noise(key_of[10], (D, FF), D ** -0.5, 0.21875, ((1, 2),))
    b_fc = noise(key_of[11], (FF,), 0.3, 2.5, ((0, 2),), jnp.float32)
    w_proj = noise(key_of[12], (FF, D), FF ** -0.5, 0.109375, ((0, 2),))
    b_proj = noise(key_of[13], (D,), 0.3, 2.5, (), jnp.float32)
    cotangent = noise(key_of[14], (TOKENS, D), 1.0, 6.0, ((0, 64),), jnp.float32)
    return dict(layer_input=layer_input, seg_ids=seg_ids, ln1_gain=ln1_gain, ln1_bias=ln1_bias, ln2_gain=ln2_gain, ln2_bias=ln2_bias, w_qkv=w_qkv, b_qkv=b_qkv, w_out=w_out, b_out=b_out, w_fc=w_fc, b_fc=b_fc, w_proj=w_proj, b_proj=b_proj, cotangent=cotangent)


@jax.custom_vjp
def low(v):
    return lax.optimization_barrier(v.astype(jnp.bfloat16)).astype(jnp.float32)

@jax.custom_vjp
def low_back(v):
    return v

def low_keep(v):
    return (low(v), None)

def low_pass(kept, grad):
    return (grad,)

def back_keep(v):
    return (v, None)

def back_low(kept, grad):
    return (low(grad),)
low.defvjp(low_keep, low_pass)
low_back.defvjp(back_keep, back_low)
highest = lax.Precision.HIGHEST
epsilon = 1e-05
masked_score = -1000000000.0

def norm_rows(row_values, gain_vec, shift_vec):
    row_mean = lax.optimization_barrier(jnp.mean(row_values, axis=-1, keepdims=True))
    centred = row_values - row_mean
    variance = lax.optimization_barrier(jnp.mean(centred * centred, axis=-1, keepdims=True))
    return centred * lax.rsqrt(variance + epsilon) * gain_vec + shift_vec

def rotate(row_values, cosine_table, sine_table):
    half_rot = ROT // 2
    leading = row_values[..., :half_rot]
    trailing = row_values[..., half_rot:ROT]
    cosine_col = cosine_table[:, None, :]
    sine_col = sine_table[:, None, :]
    return jnp.concatenate([leading * cosine_col - trailing * sine_col, trailing * cosine_col + leading * sine_col, row_values[..., ROT:]], axis=-1)

def tables(segments):
    indices = jnp.arange(SEQ, dtype=jnp.int32)
    starts = jnp.concatenate([jnp.ones((1,), dtype=bool), segments[1:] != segments[:-1]])
    opening = lax.cummax(jnp.where(starts, indices, 0), axis=0)
    offset = (indices - opening).astype(jnp.float32)
    frequency = 10000.0 ** (jnp.arange(ROT // 2).astype(jnp.float32) * (-2.0 / ROT))
    angles = offset[:, None] * frequency[None, :]
    allowed = (segments[:, None] == segments[None, :]) & (indices[:, None] >= indices[None, :])
    return (jnp.cos(angles), jnp.sin(angles), allowed)

def softmax_rows(scores):
    row_top = lax.optimization_barrier(jnp.max(scores, axis=-1, keepdims=True))
    powers = jnp.exp(scores - row_top)
    return powers / lax.optimization_barrier(jnp.sum(powers, axis=-1, keepdims=True))

def attend(packed):
    mixed_seq, segments = packed
    cosine_table, sine_table, allowed = tables(segments)
    queries = low(rotate(mixed_seq[..., :HD], cosine_table, sine_table))
    keys_rot = low(rotate(mixed_seq[..., HD:2 * HD], cosine_table, sine_table))
    values = low(mixed_seq[..., 2 * HD:])
    scores = jnp.einsum('qhd,khd->hqk', queries, keys_rot, precision=highest) * HD ** (-0.5)
    scores = low_back(jnp.where(allowed[None], scores, masked_score))
    weights = low(softmax_rows(scores))
    return jnp.einsum('hqk,khd->qhd', weights, values, precision=highest)

def block_forward(x_float, weights, seg_ids):
    ln1_gain, ln1_bias, ln2_gain, ln2_bias, w_qkv, b_qkv, w_out, b_out, w_fc, b_fc, w_proj, b_proj = weights
    normed_attn = low(norm_rows(x_float, ln1_gain, ln1_bias))
    normed_mlp = low(norm_rows(x_float, ln2_gain, ln2_bias))
    mixed_qkv = jnp.einsum('td,dhe->the', normed_attn, w_qkv, precision=highest) + b_qkv
    mixed_qkv = low_back(mixed_qkv)
    seq_count = TOKENS // SEQ
    context = lax.map(jax.checkpoint(attend), (mixed_qkv.reshape(seq_count, SEQ, H, 3 * HD), seg_ids.reshape(seq_count, SEQ)))
    context = low(low_back(context.reshape(TOKENS, H * HD)))
    attn_part = jnp.dot(context, w_out.reshape(H * HD, D), precision=highest)
    hidden = low_back(jnp.dot(normed_mlp, w_fc, precision=highest) + b_fc)
    activated = low(jax.nn.gelu(hidden, approximate=False))
    mlp_part = jnp.dot(activated, w_proj, precision=highest)
    branch = low_back(attn_part + mlp_part)
    return x_float + branch + b_out + b_proj

def reference(layer_input, seg_ids, ln1_gain, ln1_bias, ln2_gain, ln2_bias, w_qkv, b_qkv, w_out, b_out, w_fc, b_fc, w_proj, b_proj, cotangent):
    weights = (ln1_gain, ln1_bias, ln2_gain, ln2_bias, w_qkv.astype(jnp.float32), b_qkv, w_out.astype(jnp.float32), b_out, w_fc.astype(jnp.float32), b_fc, w_proj.astype(jnp.float32), b_proj)
    output, pullback = jax.vjp(lambda x_float, params: block_forward(x_float, params, seg_ids), layer_input.astype(jnp.float32), weights)
    grad_x, gradients = pullback(cotangent)
    return (output.astype(jnp.bfloat16), grad_x, gradients[0], gradients[1], gradients[2], gradients[3], gradients[4], gradients[5], gradients[6], gradients[7], gradients[8], gradients[9], gradients[10], gradients[11])
```

```python
import functools

import jax
import jax.numpy as jnp
import numpy as np
from jax import lax
from jax.experimental import pallas as pl
from jax.experimental.pallas import tpu as pltpu
from jax.sharding import PartitionSpec as P

HD = 64
ROT = 16
SEQ = 512
D = 768
FFL = 1536
EPS = 1e-05
MASKED = -1000000000.0
BF = jnp.bfloat16
F32 = jnp.float32


def place(z, x, y, c):
    return ((z * 4 + x) * 4 + y) * 2 + c


def build_perm(kind, step=1):
    pairs = []
    for z in range(2):
        for x in range(4):
            for y in range(4):
                for c in range(2):
                    if kind == "core":
                        dst = place(z, x, y, 1 - c)
                    elif kind == "z":
                        dst = place(1 - z, x, y, c)
                    elif (kind == "first") == (c == 0):
                        dst = place(z, (x + step) % 4, y, c)
                    else:
                        dst = place(z, x, (y + step) % 4, c)
                    pairs.append((place(z, x, y, c), dst))
    return pairs


CORE = build_perm("core")
ZHI = build_perm("z")
FIRST = {d: build_perm("first", d) for d in (1, 2, 3)}
SECOND = {d: build_perm("second", d) for d in (1, 2, 3)}
SWAP = [(0, 1), (1, 0)]


def move(v, perm):
    return lax.ppermute(v, "dp", perm)


def dot(a, b):
    return jnp.dot(a, b, preferred_element_type=F32)


def dot_nt(a, b):
    return lax.dot_general(a, b, (((1,), (1,)), ((), ())), preferred_element_type=F32)


def dot_tn(a, b):
    return lax.dot_general(a, b, (((0,), (0,)), ((), ())), preferred_element_type=F32)


def norm_parts(x):
    xf = x.astype(F32)
    centred = xf - jnp.mean(xf, axis=-1, keepdims=True)
    rstd = lax.rsqrt(jnp.mean(centred * centred, axis=-1, keepdims=True) + EPS)
    return centred * rstd, rstd


def mlp_kernel(first, half_ref, *refs):
    if first:
        (x_ref, cot_ref, vec_ref, bfc_ref, wfc_ref, wproj_ref,
         gw_ref, gm_ref, mo_ref, gb_ref, normed, gy) = refs
    else:
        (x_ref, cot_ref, vec_ref, bfc_ref, wfc_ref, wproj_ref, gm_in, mo_in,
         gw_ref, gm_ref, mo_ref, gb_ref, normed, gy) = refs
    i = pl.program_id(0)

    @pl.when(i == 0)
    def _():
        n, _unused = norm_parts(x_ref[...])
        normed[...] = (n * vec_ref[2:3, :] + vec_ref[3:4, :]).astype(BF)
        gy[...] = cot_ref[...].astype(BF)
        if first:
            gm_ref[...] = jnp.zeros_like(gm_ref)
            mo_ref[...] = jnp.zeros_like(mo_ref)
        else:
            gm_ref[...] = gm_in[...]
            mo_ref[...] = mo_in[...]

    wfc = wfc_ref[...]
    wproj = wproj_ref[...]
    hidden = dot(normed[...], wfc) + bfc_ref[...]
    cdf = 0.5 * (1.0 + lax.erf(hidden * np.float32(np.sqrt(0.5))))
    pdf = jnp.exp(-0.5 * hidden * hidden) * np.float32(1.0 / np.sqrt(2.0 * np.pi))
    act = (hidden * cdf).astype(BF)
    slope = cdf + hidden * pdf
    ghid = (dot_nt(gy[...], wproj) * slope).astype(BF)
    gb_ref[...] = jnp.sum(ghid.astype(F32), axis=0, keepdims=True)
    at = pl.multiple_of(i * 256, 256)
    gw_ref[0, pl.ds(at, 256), :] = dot_tn(act, gy[...]).astype(BF)
    gw_ref[1, :, pl.ds(at, 256)] = dot_tn(normed[...], ghid).astype(BF)
    gm_ref[...] += dot_nt(ghid, wfc)
    mo_ref[...] += dot(act, wproj)


def whole(shape):
    return pl.BlockSpec(shape, lambda *_: (0,) * len(shape))


def mlp_half(half, x, cot, vec, bfc, wfc, wproj, carry=None):
    tok = (SEQ, D)
    in_specs = [
        whole(tok), whole(tok), whole((8, D)),
        pl.BlockSpec((1, 256), lambda i, h: (0, h[0] * 3 + i)),
        pl.BlockSpec((D, 256), lambda i, h: (0, h[0] * 3 + i)),
        pl.BlockSpec((256, D), lambda i, h: (h[0] * 3 + i, 0)),
    ]
    args = [x, cot, vec, bfc, wfc, wproj]
    if carry is not None:
        in_specs += [whole(tok), whole(tok)]
        args += list(carry)
    return pl.pallas_call(
        functools.partial(mlp_kernel, carry is None),
        grid_spec=pltpu.PrefetchScalarGridSpec(
            num_scalar_prefetch=1,
            grid=(3,),
            in_specs=in_specs,
            out_specs=[
                whole((2, D, D)), whole(tok), whole(tok),
                pl.BlockSpec((1, 256), lambda i, h: (0, i)),
            ],
            scratch_shapes=[pltpu.VMEM(tok, BF), pltpu.VMEM(tok, BF)],
        ),
        out_shape=[
            jax.ShapeDtypeStruct((2, D, D), BF),
            jax.ShapeDtypeStruct(tok, F32),
            jax.ShapeDtypeStruct(tok, F32),
            jax.ShapeDtypeStruct((1, D), F32),
        ],
        compiler_params=pltpu.CompilerParams(
            dimension_semantics=("arbitrary",), vmem_limit_bytes=36 << 20
        ),
        cost_estimate=pl.CostEstimate(
            flops=6 * 2 * SEQ * D * D, bytes_accessed=14 << 20, transcendentals=2 * SEQ * D
        ),
        name="mlp_send" if carry is None else "mlp_keep",
    )(half, *args)


def attend_kernel(
    half_ref, x_ref, cot_ref, vec_ref, seg_ref, freq_ref, wq_ref, bq_ref, wo_ref,
    gm_ref, mo_ref, gb1_ref, gb2_ref,
    grads_ref, n1_ref, gy_ref, out_ref, gx_ref, sm_ref,
    bias, ctab, s1tab, s2tab, gn1, acc,
):
    p = pl.program_id(0)
    lane = lax.broadcasted_iota(jnp.int32, (1, 128), 1)

    @pl.when(p == 0)
    def _():
        n, _unused = norm_parts(x_ref[...])
        n1_ref[...] = (n * vec_ref[0:1, :] + vec_ref[1:2, :]).astype(BF)
        gy_ref[...] = cot_ref[...].astype(BF)
        seg_row = seg_ref[...]
        seg_col = jnp.transpose(jnp.broadcast_to(seg_row, (128, SEQ)))
        row_at = lax.broadcasted_iota(jnp.int32, (SEQ, 128), 0)
        before = jnp.zeros((SEQ, 128), F32)
        for b in range(SEQ // 128):
            seg_k = seg_row[:, b * 128 : (b + 1) * 128]
            before += jnp.where(seg_k < seg_col, 1.0, 0.0)
            k_at = lane + b * 128
            ok = (seg_k == seg_col) & (row_at >= k_at)
            bias[:, b * 128 : (b + 1) * 128] = jnp.where(ok, 0.0, MASKED)
        opening = jnp.sum(before, axis=1, keepdims=True)
        offset = row_at.astype(F32) - opening
        angle = offset * freq_ref[...]
        cosine, sine = jnp.cos(angle), jnp.sin(angle)
        j = lax.rem(lane, 64)
        ctab[...] = jnp.where(j < 16, cosine, 1.0)
        s1tab[...] = jnp.where(j < 8, -sine, 0.0)
        s2tab[...] = jnp.where((j >= 8) & (j < 16), sine, 0.0)
        gn1[...] = jnp.zeros_like(gn1)
        acc[...] = mo_ref[...]

    def rot(u, sign):
        turned = pltpu.roll(u, 120, 1) * s1tab[...] + pltpu.roll(u, 8, 1) * s2tab[...]
        return u * ctab[...] + sign * turned

    def rows(h, part):
        at = h * 192 + part * 64
        return wq_ref[at : at + 64, :]

    wp = jnp.concatenate([rows(h, part) for part in range(3) for h in range(2)], axis=0)
    n1 = n1_ref[...]
    mixed = dot_nt(n1, wp) + bq_ref[0]
    q = rot(mixed[:, :128], 1.0).astype(BF) * 0.125
    k = rot(mixed[:, 128:256], 1.0).astype(BF)
    v = mixed[:, 256:].astype(BF)
    wo = wo_ref[...]
    go = dot_nt(gy_ref[...], wo).astype(BF)
    zero = jnp.zeros((), BF)
    half_len = SEQ // 2
    ctx = [None, None]
    gq = [None, None]
    gk = [None, None]
    gv = [None, None]

    def add(slot, i, val):
        slot[i] = val if slot[i] is None else slot[i] + val

    for hh in range(2):
        mine = (lane // 64) == hh
        qm = jnp.where(mine, q, zero)
        km = jnp.where(mine, k, zero)
        vm = jnp.where(mine, v, zero)
        gom = jnp.where(mine, go, zero)
        for b in range(2):
            r = slice(b * half_len, (b + 1) * half_len)
            end = (b + 1) * half_len
            s = dot_nt(qm[r], k[:end]) + bias[r, :end]
            powers = jnp.exp(s - jnp.max(s, axis=-1, keepdims=True))
            probs = powers * (1.0 / jnp.sum(powers, axis=-1, keepdims=True))
            weights = probs.astype(BF)
            add(ctx, b, dot(weights, vm[:end]))
            gp = dot_nt(gom[r], v[:end])
            delta = jnp.sum(probs * gp, axis=-1, keepdims=True)
            gs = (probs * (gp - delta)).astype(BF)
            add(gq, b, dot(gs, km[:end]))
            for kb in range(b + 1):
                kr = slice(kb * half_len, (kb + 1) * half_len)
                add(gk, kb, dot_tn(gs[:, kr], qm[r]))
                add(gv, kb, dot_tn(weights[:, kr], gom[r]))
    ctx_all = jnp.concatenate(ctx, axis=0).astype(BF)
    gq_all = rot(jnp.concatenate(gq, axis=0) * 0.125, -1.0).astype(BF)
    gk_all = rot(jnp.concatenate(gk, axis=0), -1.0).astype(BF)
    gv_all = jnp.concatenate(gv, axis=0).astype(BF)
    parts = (gq_all, gk_all, gv_all)
    gmix = jnp.concatenate(parts, axis=1)
    gn1[...] += dot(gmix, wp)
    acc[...] += dot(ctx_all, wo)
    spots = ((0, 128, 256, 640), (384, 512, 768, 1280), (896, 1024, 1152, 1408))
    for step in range(3):

        @pl.when(p == step)
        def _(step=step):
            for at, val in zip(spots[step], parts + (ctx_all,)):
                grads_ref[:, at : at + 128] = val
            for part in range(3):
                row = 42 + step * 3 + part
                sm_ref[row : row + 1, :] = jnp.sum(
                    parts[part].astype(F32), axis=0, keepdims=True
                )

    @pl.when(p == 2)
    def _():
        out_ref[...] = acc[...].astype(BF)
        n, rstd = norm_parts(x_ref[...])
        u1, u2 = gn1[...], gm_ref[...]
        ug = u1 * vec_ref[0:1, :] + u2 * vec_ref[2:3, :]
        m1 = jnp.mean(ug, axis=-1, keepdims=True)
        m2 = jnp.mean(ug * n, axis=-1, keepdims=True)
        gx_ref[...] = ((ug - m1 - n * m2) * rstd).astype(BF)

        def put(row, vec):
            for j in range(6):
                sm_ref[pl.ds(row + j, 1), :] = vec[:, j * 128 : (j + 1) * 128]

        put(0, jnp.sum(u1 * n, axis=0, keepdims=True))
        put(6, jnp.sum(u1, axis=0, keepdims=True))
        put(12, jnp.sum(u2 * n, axis=0, keepdims=True))
        put(18, jnp.sum(u2, axis=0, keepdims=True))
        put(24, jnp.sum(cot_ref[...], axis=0, keepdims=True))
        put(30 + 6 * half_ref[0], gb1_ref[...])
        put(30 + 6 * (1 - half_ref[0]), gb2_ref[...])
        sm_ref[51:64, :] = jnp.zeros((13, 128), F32)


def attend(half, x, cot, vec, seg, freq, wq, bq, wo, gm, mo, gb1, gb2):
    tok = (SEQ, D)
    return pl.pallas_call(
        attend_kernel,
        grid_spec=pltpu.PrefetchScalarGridSpec(
            num_scalar_prefetch=1,
            grid=(3,),
            in_specs=[
                whole(tok), whole(tok), whole((8, D)), whole((1, SEQ)), whole((1, 128)),
                pl.BlockSpec((384, D), lambda p, h: (p, 0)),
                pl.BlockSpec((1, 1, 384), lambda p, h: (p, 0, 0)),
                pl.BlockSpec((128, D), lambda p, h: (p, 0)),
                whole(tok), whole(tok), whole((1, D)), whole((1, D)),
            ],
            out_specs=[
                whole((SEQ, 1536)), whole(tok), whole(tok), whole(tok), whole(tok),
                whole((64, 128)),
            ],
            scratch_shapes=[
                pltpu.VMEM((SEQ, SEQ), F32),
                pltpu.VMEM((SEQ, 128), F32),
                pltpu.VMEM((SEQ, 128), F32),
                pltpu.VMEM((SEQ, 128), F32),
                pltpu.VMEM(tok, F32),
                pltpu.VMEM(tok, F32),
            ],
        ),
        out_shape=[
            jax.ShapeDtypeStruct((SEQ, 1536), BF),
            jax.ShapeDtypeStruct(tok, BF),
            jax.ShapeDtypeStruct(tok, BF),
            jax.ShapeDtypeStruct(tok, BF),
            jax.ShapeDtypeStruct(tok, BF),
            jax.ShapeDtypeStruct((64, 128), F32),
        ],
        compiler_params=pltpu.CompilerParams(
            dimension_semantics=("arbitrary",), vmem_limit_bytes=48 << 20
        ),
        cost_estimate=pl.CostEstimate(
            flops=14 << 30, bytes_accessed=16 << 20, transcendentals=2 << 20
        ),
        name="attend",
    )(half, x, cot, vec, seg, freq, wq, bq, wo, gm, mo, gb1, gb2)


def wgrad_kernel(half_ref, g_ref, n1_ref, gy_ref, o_ref):
    i = pl.program_id(0)
    is_ctx = i >= 5 - half_ref[0]

    @pl.when(is_ctx)
    def _():
        o_ref[...] = dot_tn(g_ref[...], gy_ref[...]).astype(BF)

    @pl.when(jnp.logical_not(is_ctx))
    def _():
        o_ref[...] = dot_tn(g_ref[...], n1_ref[...]).astype(BF)


def wgrad_half(half, grads, n1, gy, name):
    tok = (SEQ, D)
    return pl.pallas_call(
        wgrad_kernel,
        grid_spec=pltpu.PrefetchScalarGridSpec(
            num_scalar_prefetch=1,
            grid=(6,),
            in_specs=[
                pl.BlockSpec((SEQ, 128), lambda i, h: (0, h[0] * 6 + i)),
                whole(tok), whole(tok),
            ],
            out_specs=pl.BlockSpec((128, D), lambda i, h: (i, 0)),
        ),
        out_shape=jax.ShapeDtypeStruct((D, D), BF),
        compiler_params=pltpu.CompilerParams(
            dimension_semantics=("arbitrary",), vmem_limit_bytes=24 << 20
        ),
        cost_estimate=pl.CostEstimate(
            flops=2 * SEQ * D * D, bytes_accessed=4 << 20, transcendentals=0
        ),
        name=name,
    )(half, grads, n1, gy)


def pick(v, index, axis):
    return lax.dynamic_index_in_dim(v, index, axis, keepdims=False)


def reduce_chunks(total, pos):
    a1, a2, z = pos
    got = [move(total((a1 + d) % 4).astype(BF), FIRST[d]) for d in (1, 3, 2)]
    own = total(a1)
    for g in got:
        own = own + g.astype(F32)
    n, _, w = own.shape
    own = own.reshape(n, 4, 48, w)
    got = [move(pick(own, (a2 + d) % 4, 1).astype(BF), SECOND[d]) for d in (1, 3, 2)]
    own = pick(own, a2, 1)
    for g in got:
        own = own + g.astype(F32)
    own = own.reshape(n, 2, 24, w)
    got = move(pick(own, 1 - z, 1).astype(BF), ZHI)
    return pick(own, z, 1) + got.astype(F32)


def gather_chunks(mine, pos):
    a1, a2, z = pos
    n, _, w = mine.shape
    other = move(mine, ZHI)
    low = jnp.where(z == 0, mine, other)
    high = jnp.where(z == 0, other, mine)
    part = jnp.stack([low, high], axis=1).reshape(n, 48, w)
    got = {d: move(part, SECOND[d]) for d in (1, 3, 2)}
    ring = jnp.stack([part, got[3], got[2], got[1]] + [part, got[3], got[2]], axis=1)
    chunk = lax.dynamic_slice_in_dim(ring, (4 - a2) % 4, 4, 1).reshape(n, 192, w)
    got = {d: move(chunk, FIRST[d]) for d in (1, 3, 2)}
    chunks = [chunk, got[1], got[2], got[3]]
    return chunks + [move(c, CORE) for c in chunks]


def unpack_mlp_kernel(pos_ref, *refs):
    chunks, (proj_ref, fc_ref), (buf, sems) = refs[:8], refs[8:10], refs[10:]
    copies = []
    for s in range(8):
        half, j = pos_ref[2 * s], pos_ref[2 * s + 1]
        buf[s] = chunks[s][...].astype(F32)
        row = pl.multiple_of(half * 768 + j * 192, 64)
        copies.append(
            pltpu.make_async_copy(buf.at[s, 0], proj_ref.at[pl.ds(row, 192), :], sems.at[s, 0])
        )
        copies[-1].start()
        row = pl.multiple_of(j * 192, 64)
        col = pl.multiple_of(half * 768, 128)
        copies.append(
            pltpu.make_async_copy(
                buf.at[s, 1], fc_ref.at[pl.ds(row, 192), pl.ds(col, 768)], sems.at[s, 1]
            )
        )
        copies[-1].start()
    for c in copies:
        c.wait()


def unpack_mlp(pos, chunks):
    return pl.pallas_call(
        unpack_mlp_kernel,
        grid_spec=pltpu.PrefetchScalarGridSpec(
            num_scalar_prefetch=1,
            grid=(1,),
            in_specs=[whole((2, 192, D))] * 8,
            out_specs=[pl.BlockSpec(memory_space=pl.ANY)] * 2,
            scratch_shapes=[
                pltpu.VMEM((8, 2, 192, D), F32),
                pltpu.SemaphoreType.DMA((8, 2)),
            ],
        ),
        out_shape=[
            jax.ShapeDtypeStruct((FFL, D), F32),
            jax.ShapeDtypeStruct((D, FFL), F32),
        ],
        compiler_params=pltpu.CompilerParams(vmem_limit_bytes=32 << 20),
        cost_estimate=pl.CostEstimate(flops=0, bytes_accessed=14 << 20, transcendentals=0),
        name="unpack_mlp",
    )(pos, *chunks)


def block_row(half, b):
    qkv_blocks = 10 - 2 * half
    is_out = b >= qkv_blocks
    out_row = (b - qkv_blocks + 2 * half) * 64
    t = b + 10 * half
    pair, within = t // 6, t % 6
    qkv_row = (pair * 2 + within % 2) * 192 + (within // 2) * 64
    return is_out, out_row, qkv_row


def unpack_attn_kernel(pos_ref, *refs):
    chunks, (qkv_ref, out_ref, sm_ref), (buf, sems) = refs[:8], refs[8:11], refs[11:]
    copies = []
    for s in range(8):
        half, j = pos_ref[2 * s], pos_ref[2 * s + 1]
        buf[s] = chunks[s][0, :, :D].astype(F32)

        @pl.when((half == 0) & (j == 0))
        def _(s=s):
            sm_ref[...] = chunks[s][0, :64, D:].astype(F32)

        for t in range(3):
            is_out, out_row, qkv_row = block_row(half, j * 3 + t)
            src = buf.at[s, pl.ds(t * 64, 64), :]
            to_out = pltpu.make_async_copy(
                src,
                out_ref.at[pl.ds(pl.multiple_of(jnp.where(is_out, out_row, 0), 64), 64), :],
                sems.at[s, t],
            )
            to_qkv = pltpu.make_async_copy(
                src,
                qkv_ref.at[pl.ds(pl.multiple_of(jnp.where(is_out, 0, qkv_row), 64), 64), :],
                sems.at[s, t],
            )

            @pl.when(is_out)
            def _(to_out=to_out):
                to_out.start()

            @pl.when(jnp.logical_not(is_out))
            def _(to_qkv=to_qkv):
                to_qkv.start()

            copies.append((is_out, to_out, to_qkv))
    for is_out, to_out, to_qkv in copies:

        @pl.when(is_out)
        def _(to_out=to_out):
            to_out.wait()

        @pl.when(jnp.logical_not(is_out))
        def _(to_qkv=to_qkv):
            to_qkv.wait()


def unpack_attn(pos, chunks):
    return pl.pallas_call(
        unpack_attn_kernel,
        grid_spec=pltpu.PrefetchScalarGridSpec(
            num_scalar_prefetch=1,
            grid=(1,),
            in_specs=[whole((1, 192, 896))] * 8,
            out_specs=[
                pl.BlockSpec(memory_space=pl.ANY),
                pl.BlockSpec(memory_space=pl.ANY),
                whole((64, 128)),
            ],
            scratch_shapes=[
                pltpu.VMEM((8, 192, D), F32),
                pltpu.SemaphoreType.DMA((8, 3)),
            ],
        ),
        out_shape=[
            jax.ShapeDtypeStruct((1152, D), F32),
            jax.ShapeDtypeStruct((384, D), F32),
            jax.ShapeDtypeStruct((64, 128), F32),
        ],
        compiler_params=pltpu.CompilerParams(vmem_limit_bytes=24 << 20),
        cost_estimate=pl.CostEstimate(flops=0, bytes_accessed=8 << 20, transcendentals=0),
        name="unpack_attn",
    )(pos, *chunks)


def body(
    layer_input, seg_ids, ln1_gain, ln1_bias, ln2_gain, ln2_bias, w_qkv, b_qkv, w_out, b_out,
    w_fc, b_fc, w_proj, b_proj, cotangent,
):
    me = lax.axis_index("dp")
    core = me % 2
    y = (me // 2) % 4
    x = (me // 8) % 4
    z = me // 32
    a1 = jnp.where(core == 0, x, y)
    a2 = jnp.where(core == 0, y, x)
    pos = (a1, a2, z)
    table = []
    for half, first in ((core, a1), (1 - core, a2)):
        for d in range(4):
            table += [half, (first - d) % 4]
    table = jnp.stack(table).astype(jnp.int32)
    keep = core.reshape(1).astype(jnp.int32)
    send = 1 - keep

    bias_sum = b_out + b_proj
    zero = jnp.zeros_like(ln1_gain)
    vec = jnp.stack([ln1_gain, ln1_bias, ln2_gain, ln2_bias, bias_sum, zero, zero, zero])
    bfc = b_fc.reshape(1, FFL)
    wq = jnp.transpose(w_qkv, (1, 2, 0)).reshape(1152, D)
    wo = w_out.reshape(384, D)
    bq = b_qkv.reshape(3, 2, 3, 64).transpose(0, 2, 1, 3).reshape(3, 1, 384)
    seg = seg_ids.astype(F32).reshape(1, SEQ)
    freq = np.float32(10000.0) ** (np.arange(ROT // 2).astype(np.float32) * np.float32(-2.0 / ROT))
    freq = jnp.asarray(np.tile(freq, 16)[None, :].astype(np.float32))

    gw_send, gm, mo, gb_send = mlp_half(send, layer_input, cotangent, vec, bfc, w_fc, w_proj)
    gw_recv = move(gw_send, CORE).reshape(2, 4, 192, D)
    gw_keep, gm, mo, gb_keep = mlp_half(
        keep, layer_input, cotangent, vec, bfc, w_fc, w_proj, (gm, mo)
    )
    gw_keep = gw_keep.reshape(2, 4, 192, D)

    def mlp_total(j):
        return pick(gw_keep, j, 1).astype(F32) + pick(gw_recv, j, 1).astype(F32)

    mlp_mine = reduce_chunks(mlp_total, pos).astype(BF)

    grads, n1, gy, out_part, gx_part, small = attend(
        send, layer_input, cotangent, vec, seg, freq, wq, bq, wo, gm, mo, gb_send, gb_keep
    )
    norms = small[:24] + lax.ppermute(small[:24], "tensor", SWAP)
    small = jnp.concatenate([norms, small[24:]], axis=0)
    small = small + move(small, CORE)
    aw_send = wgrad_half(send, grads, n1, gy, "wgrad_send")
    aw_recv = move(aw_send, CORE).reshape(1, 4, 192, D)
    aw_keep = wgrad_half(keep, grads, n1, gy, "wgrad_keep").reshape(1, 4, 192, D)
    small_rows = jnp.pad(small, ((0, 128), (0, 0)))[None]

    def attn_total(j):
        main = pick(aw_keep, j, 1).astype(F32) + pick(aw_recv, j, 1).astype(F32)
        return jnp.concatenate([main, jnp.where(j == 0, small_rows, 0.0)], axis=2)

    attn_mine = reduce_chunks(attn_total, pos).astype(BF)

    out_other = lax.ppermute(out_part, "tensor", SWAP)
    gx_other = lax.ppermute(gx_part, "tensor", SWAP)
    output = (
        layer_input.astype(F32) + (out_part.astype(F32) + out_other.astype(F32)) + bias_sum
    ).astype(BF)
    grad_x = cotangent + (gx_part.astype(F32) + gx_other.astype(F32))

    g_proj, g_fc = unpack_mlp(table, gather_chunks(mlp_mine, pos))
    g_qkv, g_out, sm = unpack_attn(table, gather_chunks(attn_mine, pos))
    g_qkv = jnp.transpose(g_qkv.reshape(6, 192, D), (2, 0, 1))
    g_out = g_out.reshape(6, 64, D)
    vecs = [sm[6 * i : 6 * i + 6].reshape(D) for i in range(5)]
    g_bfc = sm[30:42].reshape(FFL)
    g_bqkv = sm[42:51].reshape(3, 3, 2, 64).transpose(0, 2, 1, 3).reshape(6, 192)
    return (
        output, grad_x, vecs[0], vecs[1], vecs[2], vecs[3], g_qkv, g_bqkv, g_out, vecs[4],
        g_fc, g_bfc, g_proj, vecs[4],
    )


def solution(mesh):
    placed = (
        P("dp", None), P("dp"), P(), P(), P(), P(),
        P(None, "tensor", None), P("tensor", None), P("tensor", None, None), P(),
        P(None, "tensor"), P("tensor"), P("tensor", None), P(), P("dp", None),
    )
    return jax.shard_map(
        body,
        mesh=mesh,
        in_specs=placed,
        out_specs=(
            P("dp", None), P("dp", None), P(), P(), P(), P(),
            P(None, "tensor", None), P("tensor", None), P("tensor", None, None), P(),
            P(None, "tensor"), P("tensor"), P("tensor", None), P(),
        ),
        check_vma=False,
    )
```

```python
import functools

import jax
import jax.numpy as jnp
import numpy as np
from jax import lax
from jax.experimental import pallas as pl
from jax.experimental.pallas import tpu as pltpu
from jax.sharding import PartitionSpec as P

HD = 64
ROT = 16
SEQ = 512
D = 768
FFL = 1536
EPS = 1e-05
MASKED = -1000000000.0
BF = jnp.bfloat16
F32 = jnp.float32


def place(z, x, y, c):
    return ((z * 4 + x) * 4 + y) * 2 + c


def build_perm(kind, step=1):
    pairs = []
    for z in range(2):
        for x in range(4):
            for y in range(4):
                for c in range(2):
                    if kind == "core":
                        dst = place(z, x, y, 1 - c)
                    elif kind == "z":
                        dst = place(1 - z, x, y, c)
                    elif (kind == "first") == (c == 0):
                        dst = place(z, (x + step) % 4, y, c)
                    else:
                        dst = place(z, x, (y + step) % 4, c)
                    pairs.append((place(z, x, y, c), dst))
    return pairs


CORE = build_perm("core")
ZHI = build_perm("z")
FIRST = {d: build_perm("first", d) for d in (1, 2, 3)}
SECOND = {d: build_perm("second", d) for d in (1, 2, 3)}
SWAP = [(0, 1), (1, 0)]


def move(v, perm):
    return lax.ppermute(v, "dp", perm)


def dot(a, b):
    return jnp.dot(a, b, preferred_element_type=F32)


def dot_nt(a, b):
    return lax.dot_general(a, b, (((1,), (1,)), ((), ())), preferred_element_type=F32)


def dot_tn(a, b):
    return lax.dot_general(a, b, (((0,), (0,)), ((), ())), preferred_element_type=F32)


def norm_parts(x):
    xf = x.astype(F32)
    centred = xf - jnp.mean(xf, axis=-1, keepdims=True)
    rstd = lax.rsqrt(jnp.mean(centred * centred, axis=-1, keepdims=True) + EPS)
    return centred * rstd, rstd


def mlp_kernel(first, half_ref, *refs):
    if first:
        (x_ref, cot_ref, g_ref, b_ref, bfc_ref, wfc_ref, wproj_ref,
         gw_ref, gm_ref, mo_ref, gb_ref, normed, gy) = refs
    else:
        (x_ref, cot_ref, g_ref, b_ref, bfc_ref, wfc_ref, wproj_ref, gm_in, mo_in,
         gw_ref, gm_ref, mo_ref, gb_ref, normed, gy) = refs
    i = pl.program_id(0)

    @pl.when(i == 0)
    def _():
        n, _unused = norm_parts(x_ref[...])
        normed[...] = (n * as_row(g_ref) + as_row(b_ref)).astype(BF)
        gy[...] = cot_ref[...].astype(BF)
        if first:
            gm_ref[...] = jnp.zeros_like(gm_ref)
            mo_ref[...] = jnp.zeros_like(mo_ref)
        else:
            gm_ref[...] = gm_in[...]
            mo_ref[...] = mo_in[...]

    wfc = wfc_ref[...]
    wproj = wproj_ref[...]
    hidden = dot(normed[...], wfc) + bfc_ref[:, pl.ds(pl.multiple_of((half_ref[0] * 3 + i) * 256, 256), 256)]
    cdf = 0.5 * (1.0 + lax.erf(hidden * np.float32(np.sqrt(0.5))))
    pdf = jnp.exp(-0.5 * hidden * hidden) * np.float32(1.0 / np.sqrt(2.0 * np.pi))
    act = (hidden * cdf).astype(BF)
    slope = cdf + hidden * pdf
    ghid = (dot_nt(gy[...], wproj) * slope).astype(BF)
    gb_ref[...] = jnp.sum(ghid.astype(F32), axis=0, keepdims=True)
    at = pl.multiple_of(i * 256, 256)
    gw_ref[0, pl.ds(at, 256), :] = dot_tn(act, gy[...]).astype(BF)
    gw_ref[1, :, pl.ds(at, 256)] = dot_tn(normed[...], ghid).astype(BF)
    gm_ref[...] += dot_nt(ghid, wfc)
    mo_ref[...] += dot(act, wproj)


def whole(shape):
    return pl.BlockSpec(shape, lambda *_: (0,) * len(shape))


def as_row(ref):
    return ref[...].reshape(1, ref.shape[0])


def in_hbm(*arrays):
    return [pltpu.with_memory_space_constraint(v, pltpu.HBM) for v in arrays]


def mlp_half(half, x, cot, gain, shift, bfc, wfc, wproj, carry=None):
    tok = (SEQ, D)
    in_specs = [
        whole(tok), whole(tok), whole((D,)), whole((D,)), whole((1, FFL)),
        pl.BlockSpec((D, 256), lambda i, h: (0, h[0] * 3 + i)),
        pl.BlockSpec((256, D), lambda i, h: (h[0] * 3 + i, 0)),
    ]
    x, cot, wfc, wproj = in_hbm(x, cot, wfc, wproj)
    args = [x, cot, gain, shift, bfc, wfc, wproj]
    if carry is not None:
        in_specs += [whole(tok), whole(tok)]
        args += list(carry)
    return pl.pallas_call(
        functools.partial(mlp_kernel, carry is None),
        grid_spec=pltpu.PrefetchScalarGridSpec(
            num_scalar_prefetch=1,
            grid=(3,),
            in_specs=in_specs,
            out_specs=[
                whole((2, D, D)), whole(tok), whole(tok),
                pl.BlockSpec((1, 256), lambda i, h: (0, i)),
            ],
            scratch_shapes=[pltpu.VMEM(tok, BF), pltpu.VMEM(tok, BF)],
        ),
        out_shape=[
            jax.ShapeDtypeStruct((2, D, D), BF),
            jax.ShapeDtypeStruct(tok, F32),
            jax.ShapeDtypeStruct(tok, F32),
            jax.ShapeDtypeStruct((1, D), F32),
        ],
        compiler_params=pltpu.CompilerParams(
            dimension_semantics=("arbitrary",), vmem_limit_bytes=36 << 20
        ),
        cost_estimate=pl.CostEstimate(
            flops=6 * 2 * SEQ * D * D, bytes_accessed=14 << 20, transcendentals=2 * SEQ * D
        ),
        name="mlp_send" if carry is None else "mlp_keep",
    )(half, *args)


def attend_kernel(
    half_ref, x_ref, cot_ref, g1_ref, b1_ref, g2_ref, seg_ref, freq_ref, wq_ref, bq_ref, wo_ref,
    gm_ref, mo_ref, gb1_ref, gb2_ref,
    grads_ref, n1_ref, gy_ref, out_ref, gx_ref, sm_ref,
    bias, ctab, s1tab, s2tab, gn1, acc,
):
    p = pl.program_id(0)
    lane = lax.broadcasted_iota(jnp.int32, (1, 128), 1)

    @pl.when(p == 0)
    def _():
        n, _unused = norm_parts(x_ref[...])
        n1_ref[...] = (n * as_row(g1_ref) + as_row(b1_ref)).astype(BF)
        gy_ref[...] = cot_ref[...].astype(BF)
        seg_row = as_row(seg_ref).astype(F32)
        seg_col = jnp.transpose(jnp.broadcast_to(seg_row, (128, SEQ)))
        row_at = lax.broadcasted_iota(jnp.int32, (SEQ, 128), 0)
        before = jnp.zeros((SEQ, 128), F32)
        for b in range(SEQ // 128):
            seg_k = seg_row[:, b * 128 : (b + 1) * 128]
            before += jnp.where(seg_k < seg_col, 1.0, 0.0)
            k_at = lane + b * 128
            ok = (seg_k == seg_col) & (row_at >= k_at)
            bias[:, b * 128 : (b + 1) * 128] = jnp.where(ok, 0.0, MASKED)
        opening = jnp.sum(before, axis=1, keepdims=True)
        offset = row_at.astype(F32) - opening
        angle = offset * freq_ref[...]
        cosine, sine = jnp.cos(angle), jnp.sin(angle)
        j = lax.rem(lane, 64)
        ctab[...] = jnp.where(j < 16, cosine, 1.0)
        s1tab[...] = jnp.where(j < 8, -sine, 0.0)
        s2tab[...] = jnp.where((j >= 8) & (j < 16), sine, 0.0)
        gn1[...] = jnp.zeros_like(gn1)
        acc[...] = mo_ref[...]

    def rot(u, sign):
        turned = pltpu.roll(u, 120, 1) * s1tab[...] + pltpu.roll(u, 8, 1) * s2tab[...]
        return u * ctab[...] + sign * turned

    def rows(h, part):
        at = h * 192 + part * 64
        return wq_ref[at : at + 64, :]

    wp = jnp.concatenate([rows(h, part) for part in range(3) for h in range(2)], axis=0)
    n1 = n1_ref[...]
    head = lax.broadcasted_iota(jnp.int32, (6, 192), 0)
    shifts = [
        jnp.sum(jnp.where(head == 2 * p + h, bq_ref[...], 0.0), axis=0, keepdims=True)
        for h in range(2)
    ]
    shift = jnp.concatenate(
        [shifts[h][:, part * 64 : part * 64 + 64] for part in range(3) for h in range(2)], axis=1
    )
    mixed = dot_nt(n1, wp) + shift
    q = rot(mixed[:, :128], 1.0).astype(BF) * 0.125
    k = rot(mixed[:, 128:256], 1.0).astype(BF)
    v = mixed[:, 256:].astype(BF)
    wo = wo_ref[...]
    go = dot_nt(gy_ref[...], wo).astype(BF)
    zero = jnp.zeros((), BF)
    half_len = SEQ // 2
    ctx = [None, None]
    gq = [None, None]
    gk = [None, None]
    gv = [None, None]

    def add(slot, i, val):
        slot[i] = val if slot[i] is None else slot[i] + val

    for hh in range(2):
        mine = (lane // 64) == hh
        qm = jnp.where(mine, q, zero)
        km = jnp.where(mine, k, zero)
        vm = jnp.where(mine, v, zero)
        gom = jnp.where(mine, go, zero)
        for b in range(2):
            r = slice(b * half_len, (b + 1) * half_len)
            end = (b + 1) * half_len
            s = dot_nt(qm[r], k[:end]) + bias[r, :end]
            powers = jnp.exp(s - jnp.max(s, axis=-1, keepdims=True))
            probs = powers * (1.0 / jnp.sum(powers, axis=-1, keepdims=True))
            weights = probs.astype(BF)
            add(ctx, b, dot(weights, vm[:end]))
            gp = dot_nt(gom[r], v[:end])
            delta = jnp.sum(probs * gp, axis=-1, keepdims=True)
            gs = (probs * (gp - delta)).astype(BF)
            add(gq, b, dot(gs, km[:end]))
            for kb in range(b + 1):
                kr = slice(kb * half_len, (kb + 1) * half_len)
                add(gk, kb, dot_tn(gs[:, kr], qm[r]))
                add(gv, kb, dot_tn(weights[:, kr], gom[r]))
    ctx_all = jnp.concatenate(ctx, axis=0).astype(BF)
    gq_all = rot(jnp.concatenate(gq, axis=0) * 0.125, -1.0).astype(BF)
    gk_all = rot(jnp.concatenate(gk, axis=0), -1.0).astype(BF)
    gv_all = jnp.concatenate(gv, axis=0).astype(BF)
    parts = (gq_all, gk_all, gv_all)
    gmix = jnp.concatenate(parts, axis=1)
    gn1[...] += dot(gmix, wp)
    acc[...] += dot(ctx_all, wo)
    spots = ((0, 128, 256, 640), (384, 512, 768, 1280), (896, 1024, 1152, 1408))
    for step in range(3):

        @pl.when(p == step)
        def _(step=step):
            for at, val in zip(spots[step], parts + (ctx_all,)):
                grads_ref[:, at : at + 128] = val
            for part in range(3):
                row = 42 + step * 3 + part
                sm_ref[row : row + 1, :] = jnp.sum(
                    parts[part].astype(F32), axis=0, keepdims=True
                )

    @pl.when(p == 2)
    def _():
        out_ref[...] = acc[...].astype(BF)
        n, rstd = norm_parts(x_ref[...])
        u1, u2 = gn1[...], gm_ref[...]
        ug = u1 * as_row(g1_ref) + u2 * as_row(g2_ref)
        m1 = jnp.mean(ug, axis=-1, keepdims=True)
        m2 = jnp.mean(ug * n, axis=-1, keepdims=True)
        gx_ref[...] = ((ug - m1 - n * m2) * rstd).astype(BF)

        def put(row, vec):
            for j in range(6):
                sm_ref[pl.ds(row + j, 1), :] = vec[:, j * 128 : (j + 1) * 128]

        put(0, jnp.sum(u1 * n, axis=0, keepdims=True))
        put(6, jnp.sum(u1, axis=0, keepdims=True))
        put(12, jnp.sum(u2 * n, axis=0, keepdims=True))
        put(18, jnp.sum(u2, axis=0, keepdims=True))
        put(24, jnp.sum(cot_ref[...], axis=0, keepdims=True))
        put(30 + 6 * half_ref[0], gb1_ref[...])
        put(30 + 6 * (1 - half_ref[0]), gb2_ref[...])
        sm_ref[51:64, :] = jnp.zeros((13, 128), F32)


def attend(half, x, cot, g1, b1, g2, seg, freq, wq, bq, wo, gm, mo, gb1, gb2):
    tok = (SEQ, D)
    x, cot, wq, wo = in_hbm(x, cot, wq, wo)
    return pl.pallas_call(
        attend_kernel,
        grid_spec=pltpu.PrefetchScalarGridSpec(
            num_scalar_prefetch=1,
            grid=(3,),
            in_specs=[
                whole(tok), whole(tok), whole((D,)), whole((D,)), whole((D,)), whole((SEQ,)),
                whole((1, 128)),
                pl.BlockSpec((384, D), lambda p, h: (p, 0)),
                whole((6, 192)),
                pl.BlockSpec((128, D), lambda p, h: (p, 0)),
                whole(tok), whole(tok), whole((1, D)), whole((1, D)),
            ],
            out_specs=[
                whole((SEQ, 1536)), whole(tok), whole(tok), whole(tok), whole(tok),
                whole((64, 128)),
            ],
            scratch_shapes=[
                pltpu.VMEM((SEQ, SEQ), F32),
                pltpu.VMEM((SEQ, 128), F32),
                pltpu.VMEM((SEQ, 128), F32),
                pltpu.VMEM((SEQ, 128), F32),
                pltpu.VMEM(tok, F32),
                pltpu.VMEM(tok, F32),
            ],
        ),
        out_shape=[
            jax.ShapeDtypeStruct((SEQ, 1536), BF),
            jax.ShapeDtypeStruct(tok, BF),
            jax.ShapeDtypeStruct(tok, BF),
            jax.ShapeDtypeStruct(tok, BF),
            jax.ShapeDtypeStruct(tok, BF),
            jax.ShapeDtypeStruct((64, 128), F32),
        ],
        compiler_params=pltpu.CompilerParams(
            dimension_semantics=("arbitrary",), vmem_limit_bytes=48 << 20
        ),
        cost_estimate=pl.CostEstimate(
            flops=14 << 30, bytes_accessed=16 << 20, transcendentals=2 << 20
        ),
        name="attend",
    )(half, x, cot, g1, b1, g2, seg, freq, wq, bq, wo, gm, mo, gb1, gb2)


def wgrad_kernel(half_ref, g_ref, n1_ref, gy_ref, o_ref):
    i = pl.program_id(0)
    is_ctx = i >= 5 - half_ref[0]

    @pl.when(is_ctx)
    def _():
        o_ref[...] = dot_tn(g_ref[...], gy_ref[...]).astype(BF)

    @pl.when(jnp.logical_not(is_ctx))
    def _():
        o_ref[...] = dot_tn(g_ref[...], n1_ref[...]).astype(BF)


def wgrad_half(half, grads, n1, gy, name):
    tok = (SEQ, D)
    return pl.pallas_call(
        wgrad_kernel,
        grid_spec=pltpu.PrefetchScalarGridSpec(
            num_scalar_prefetch=1,
            grid=(6,),
            in_specs=[
                pl.BlockSpec((SEQ, 128), lambda i, h: (0, h[0] * 6 + i)),
                whole(tok), whole(tok),
            ],
            out_specs=pl.BlockSpec((128, D), lambda i, h: (i, 0)),
        ),
        out_shape=jax.ShapeDtypeStruct((D, D), BF),
        compiler_params=pltpu.CompilerParams(
            dimension_semantics=("arbitrary",), vmem_limit_bytes=24 << 20
        ),
        cost_estimate=pl.CostEstimate(
            flops=2 * SEQ * D * D, bytes_accessed=4 << 20, transcendentals=0
        ),
        name=name,
    )(half, grads, n1, gy)


def pick(v, index, axis):
    return lax.dynamic_index_in_dim(v, index, axis, keepdims=False)


class Ordered:
    def __init__(self):
        self.token = None

    def __call__(self, fn, *args):
        if self.token is not None:
            args, _unused = lax.optimization_barrier((args, self.token))
        out = fn(*args)
        self.token = jax.tree.leaves(out)[0]
        return out


def split_first(total, a1):
    sends = [total((a1 + d) % 4).astype(BF) for d in (1, 3, 2)]
    return sends, total(a1)


def split_second(own, got, a2):
    for g in got:
        own = own + g.astype(F32)
    n, _, w = own.shape
    own = own.reshape(n, 4, 48, w)
    return [pick(own, (a2 + d) % 4, 1).astype(BF) for d in (1, 3, 2)], pick(own, a2, 1)


def split_z(own, got, z):
    for g in got:
        own = own + g.astype(F32)
    n, _, w = own.shape
    own = own.reshape(n, 2, 24, w)
    return pick(own, 1 - z, 1).astype(BF), pick(own, z, 1)


def finish_sum(own, got):
    return (own + got.astype(F32)).astype(BF)


def join_z(mine, other, z):
    n, _, w = mine.shape
    low = jnp.where(z == 0, mine, other)
    high = jnp.where(z == 0, other, mine)
    return jnp.stack([low, high], axis=1).reshape(n, 48, w)


def join_second(part, got, a2):
    n, _, w = part.shape
    g1, g3, g2 = got
    ring = jnp.stack([part, g3, g2, g1, part, g3, g2], axis=1)
    return lax.dynamic_slice_in_dim(ring, (4 - a2) % 4, 4, 1).reshape(n, 192, w)


def send_first(parts):
    return [move(v, FIRST[d]) for v, d in zip(parts, (1, 3, 2))]


def send_second(parts):
    return [move(v, SECOND[d]) for v, d in zip(parts, (1, 3, 2))]


def unpack_mlp_kernel(pos_ref, *refs):
    chunks, (proj_ref, fc_ref), (buf, sems) = refs[:8], refs[8:10], refs[10:]
    copies = []
    for s in range(8):
        half, j = pos_ref[2 * s], pos_ref[2 * s + 1]
        buf[s] = chunks[s][...].astype(F32)
        row = pl.multiple_of(half * 768 + j * 192, 64)
        copies.append(
            pltpu.make_async_copy(buf.at[s, 0], proj_ref.at[pl.ds(row, 192), :], sems.at[s, 0])
        )
        copies[-1].start()
        row = pl.multiple_of(j * 192, 64)
        col = pl.multiple_of(half * 768, 128)
        copies.append(
            pltpu.make_async_copy(
                buf.at[s, 1], fc_ref.at[pl.ds(row, 192), pl.ds(col, 768)], sems.at[s, 1]
            )
        )
        copies[-1].start()
    for c in copies:
        c.wait()


def unpack_mlp(pos, chunks):
    return pl.pallas_call(
        unpack_mlp_kernel,
        grid_spec=pltpu.PrefetchScalarGridSpec(
            num_scalar_prefetch=1,
            grid=(1,),
            in_specs=[whole((2, 192, D))] * 8,
            out_specs=[pl.BlockSpec(memory_space=pl.ANY)] * 2,
            scratch_shapes=[
                pltpu.VMEM((8, 2, 192, D), F32),
                pltpu.SemaphoreType.DMA((8, 2)),
            ],
        ),
        out_shape=[
            jax.ShapeDtypeStruct((FFL, D), F32),
            jax.ShapeDtypeStruct((D, FFL), F32),
        ],
        compiler_params=pltpu.CompilerParams(vmem_limit_bytes=32 << 20),
        cost_estimate=pl.CostEstimate(flops=0, bytes_accessed=14 << 20, transcendentals=0),
        name="unpack_mlp",
    )(pos, *chunks)


def block_row(half, b):
    qkv_blocks = 10 - 2 * half
    is_out = b >= qkv_blocks
    out_row = (b - qkv_blocks + 2 * half) * 64
    t = b + 10 * half
    pair, within = t // 6, t % 6
    qkv_row = (pair * 2 + within % 2) * 192 + (within // 2) * 64
    return is_out, out_row, qkv_row


def unpack_attn_kernel(pos_ref, *refs):
    chunks, (qkv_ref, out_ref, sm_ref), (buf, sems) = refs[:8], refs[8:11], refs[11:]
    copies = []
    for s in range(8):
        half, j = pos_ref[2 * s], pos_ref[2 * s + 1]
        buf[s] = chunks[s][0, :, :D].astype(F32)

        @pl.when((half == 0) & (j == 0))
        def _(s=s):
            sm_ref[...] = chunks[s][0, :64, D:].astype(F32)

        for t in range(3):
            is_out, out_row, qkv_row = block_row(half, j * 3 + t)
            src = buf.at[s, pl.ds(t * 64, 64), :]
            to_out = pltpu.make_async_copy(
                src,
                out_ref.at[pl.ds(pl.multiple_of(jnp.where(is_out, out_row, 0), 64), 64), :],
                sems.at[s, t],
            )
            to_qkv = pltpu.make_async_copy(
                src,
                qkv_ref.at[pl.ds(pl.multiple_of(jnp.where(is_out, 0, qkv_row), 64), 64), :],
                sems.at[s, t],
            )

            @pl.when(is_out)
            def _(to_out=to_out):
                to_out.start()

            @pl.when(jnp.logical_not(is_out))
            def _(to_qkv=to_qkv):
                to_qkv.start()

            copies.append((is_out, to_out, to_qkv))
    for is_out, to_out, to_qkv in copies:

        @pl.when(is_out)
        def _(to_out=to_out):
            to_out.wait()

        @pl.when(jnp.logical_not(is_out))
        def _(to_qkv=to_qkv):
            to_qkv.wait()


def unpack_attn(pos, chunks):
    return pl.pallas_call(
        unpack_attn_kernel,
        grid_spec=pltpu.PrefetchScalarGridSpec(
            num_scalar_prefetch=1,
            grid=(1,),
            in_specs=[whole((1, 192, 896))] * 8,
            out_specs=[
                pl.BlockSpec(memory_space=pl.ANY),
                pl.BlockSpec(memory_space=pl.ANY),
                whole((64, 128)),
            ],
            scratch_shapes=[
                pltpu.VMEM((8, 192, D), F32),
                pltpu.SemaphoreType.DMA((8, 3)),
            ],
        ),
        out_shape=[
            jax.ShapeDtypeStruct((1152, D), F32),
            jax.ShapeDtypeStruct((384, D), F32),
            jax.ShapeDtypeStruct((64, 128), F32),
        ],
        compiler_params=pltpu.CompilerParams(vmem_limit_bytes=24 << 20),
        cost_estimate=pl.CostEstimate(flops=0, bytes_accessed=8 << 20, transcendentals=0),
        name="unpack_attn",
    )(pos, *chunks)


def body(
    layer_input, seg_ids, ln1_gain, ln1_bias, ln2_gain, ln2_bias, w_qkv, b_qkv, w_out, b_out,
    w_fc, b_fc, w_proj, b_proj, cotangent,
):
    me = lax.axis_index("dp")
    core = me % 2
    y = (me // 2) % 4
    x = (me // 8) % 4
    z = me // 32
    a1 = jnp.where(core == 0, x, y)
    a2 = jnp.where(core == 0, y, x)
    pos = (a1, a2, z)
    table = []
    for half, first in ((core, a1), (1 - core, a2)):
        for d in range(4):
            table += [half, (first - d) % 4]
    table = jnp.stack(table).astype(jnp.int32)
    keep = core.reshape(1).astype(jnp.int32)
    send = 1 - keep

    bfc = b_fc.reshape(1, FFL)
    wq = jnp.transpose(w_qkv, (1, 2, 0)).reshape(1152, D)
    wo = w_out.reshape(384, D)
    freq = np.float32(10000.0) ** (np.arange(ROT // 2).astype(np.float32) * np.float32(-2.0 / ROT))
    freq = jnp.asarray(np.tile(freq, 16)[None, :].astype(np.float32))

    run = Ordered()
    gw_send, gm, mo, gb_send = run(
        functools.partial(mlp_half, send), layer_input, cotangent, ln2_gain, ln2_bias, bfc, w_fc, w_proj
    )
    gw_recv = move(gw_send, CORE).reshape(2, 4, 192, D)
    gw_keep, gm, mo, gb_keep = run(
        functools.partial(mlp_half, keep), layer_input, cotangent, ln2_gain, ln2_bias, bfc, w_fc, w_proj, (gm, mo)
    )
    gw_keep = gw_keep.reshape(2, 4, 192, D)

    def mlp_first(kept, recv):
        return split_first(
            lambda j: pick(kept, j, 1).astype(F32) + pick(recv, j, 1).astype(F32), a1
        )

    sends, m_own = run(mlp_first, gw_keep, gw_recv)
    m_got = send_first(sends)

    grads, n1, gy, out_part, gx_part, small = run(
        functools.partial(attend, send),
        layer_input, cotangent, ln1_gain, ln1_bias, ln2_gain, seg_ids, freq, wq, b_qkv, wo, gm, mo, gb_send, gb_keep,
    )
    norms_other = lax.ppermute(small[:24], "tensor", SWAP)

    sends, m_own = run(lambda o, g: split_second(o, g, a2), m_own, m_got)
    m_got = send_second(sends)

    aw_send = run(lambda *v: wgrad_half(send, *v, "wgrad_send"), grads, n1, gy)
    aw_recv = move(aw_send, CORE).reshape(1, 4, 192, D)

    m_send, m_own = run(lambda o, g: split_z(o, g, z), m_own, m_got)
    m_got = move(m_send, ZHI)

    small = run(lambda s, o: jnp.concatenate([s[:24] + o, s[24:]], axis=0), small, norms_other)
    small_other = move(small, CORE)
    aw_keep = run(lambda *v: wgrad_half(keep, *v, "wgrad_keep"), grads, n1, gy)
    aw_keep = aw_keep.reshape(1, 4, 192, D)

    def attn_first(kept, recv, s, o):
        rows = jnp.pad(s + o, ((0, 128), (0, 0)))[None]

        def total(j):
            main = pick(kept, j, 1).astype(F32) + pick(recv, j, 1).astype(F32)
            return jnp.concatenate([main, jnp.where(j == 0, rows, 0.0)], axis=2)

        return split_first(total, a1)

    mine = run(finish_sum, m_own, m_got)
    m_other = move(mine, ZHI)
    sends, t_own = run(attn_first, aw_keep, aw_recv, small, small_other)
    t_got = send_first(sends)

    part = run(lambda m, o: join_z(m, o, z), mine, m_other)
    m_got = send_second([part] * 3)
    out_part = run(lambda v: v, out_part)
    out_other = lax.ppermute(out_part, "tensor", SWAP)

    sends, t_own = run(lambda o, g: split_second(o, g, a2), t_own, t_got)
    t_got = send_second(sends)

    chunk = run(lambda p, g: join_second(p, g, a2), part, m_got)
    m_got = send_first([chunk] * 3)
    m_chunks = [chunk, m_got[0], m_got[2], m_got[1]]

    t_send, t_own = run(lambda o, g: split_z(o, g, z), t_own, t_got)
    t_got = move(t_send, ZHI)

    mine = run(finish_sum, t_own, t_got)
    t_other = move(mine, ZHI)
    part = run(lambda m, o: join_z(m, o, z), mine, t_other)
    t_got = send_second([part] * 3)
    gx_part = run(lambda v: v, gx_part)
    gx_other = lax.ppermute(gx_part, "tensor", SWAP)

    chunk = run(lambda p, g: join_second(p, g, a2), part, t_got)
    t_got = send_first([chunk] * 3)
    t_chunks = [chunk, t_got[0], t_got[2], t_got[1]]

    output = run(
        lambda x, p, o: (
            x.astype(F32) + (p.astype(F32) + o.astype(F32)) + b_out + b_proj
        ).astype(BF),
        layer_input, out_part, out_other,
    )

    m_chunks = m_chunks + [move(v, CORE) for v in m_chunks]
    g_proj, g_fc = run(lambda *v: unpack_mlp(table, v), *m_chunks)
    t_chunks = t_chunks + [move(v, CORE) for v in t_chunks]
    grad_x = run(
        lambda c, p, o: c + (p.astype(F32) + o.astype(F32)), cotangent, gx_part, gx_other
    )

    g_qkv, g_out, sm = run(lambda *v: unpack_attn(table, v), *t_chunks)
    g_qkv = jnp.transpose(g_qkv.reshape(6, 192, D), (2, 0, 1))
    g_out = g_out.reshape(6, 64, D)
    vecs = [sm[6 * i : 6 * i + 6].reshape(D) for i in range(5)]
    g_bfc = sm[30:42].reshape(FFL)
    g_bqkv = sm[42:51].reshape(3, 3, 2, 64).transpose(0, 2, 1, 3).reshape(6, 192)
    return (
        output, grad_x, vecs[0], vecs[1], vecs[2], vecs[3], g_qkv, g_bqkv, g_out, vecs[4],
        g_fc, g_bfc, g_proj, vecs[4],
    )


def solution(mesh):
    placed = (
        P("dp", None), P("dp"), P(), P(), P(), P(),
        P(None, "tensor", None), P("tensor", None), P("tensor", None, None), P(),
        P(None, "tensor"), P("tensor"), P("tensor", None), P(), P("dp", None),
    )
    return jax.shard_map(
        body,
        mesh=mesh,
        in_specs=placed,
        out_specs=(
            P("dp", None), P("dp", None), P(), P(), P(), P(),
            P(None, "tensor", None), P("tensor", None), P("tensor", None, None), P(),
            P(None, "tensor"), P("tensor"), P("tensor", None), P(),
        ),
        check_vma=False,
    )
```
